32 devices in a mesh: groups: 2 (over x), sect: 16 (over z, y, core).
Axes of the slice: x: 2, y: 2, z: 4, core: 2. Of those that a mesh axis runs over, the one named last changes fastest.
Arguments:
- psi: float32 [512, 128, 128], P(('groups', 'sect')), parts along dimension 0, may hold values from -120 to 120
- left_env: float32 [32, 32, 128, 128], P(('groups', 'sect')), parts along dimension 0, may hold values from -4 to 7
- right_env: float32 [32, 32, 128, 128], P(('groups', 'sect')), parts along dimension 0, may hold values from -4 to 7
- right_sector: int32 [512], P(('groups', 'sect')), parts along dimension 0, may hold values from 0 to 15, as said below
- mpo_pairs: int32 [64, 2], replicated, may hold values from 0 to 31
- mpo_coef: float32 [64], replicated, may hold values from 0 to 0.03125
Outputs:
- hpsi: float32 [512, 128, 128], P(('groups', 'sect')), parts along dimension 0
- residual: float32 [512, 128, 128], P(('groups', 'sect')), parts along dimension 0
The draws below stay inside these ranges and needn't reach their ends.
There are 2 independent parts, one for each index of `groups`. The reference program is written for one: setup_inputs(seed, part) draws one part's arguments, and reference() takes and returns one part's arrays. A program takes and returns all parts, laid end to end along the dimension named above; an argument that names none is the same for every part. Nothing has to cross between parts.
Inputs may be any that keep to these rules, and one draw needn't show every extreme that they name: `right_sector`: the right sector of block k differs from its left sector k // 16 by at most one. Among the 16 blocks of one left sector at most 2 have right sector one higher and at most 2 one lower; some sector has exactly 2 of each, and every sector that has a higher or lower neighbour has at least one block going to it.
All inputs are finite; a program needn't handle non-finite values.
Results may differ from the reference program's by a relative error of at most 0.0003.
Values sent between devices are 32-bit elements; how exact they have to be, the bound alone decides.
A program may use at most 192 MiB of HBM per device.

```python
import math
import jax
import jax.numpy as jnp
from jax import lax

BS = 128
DW = 32
NPAIR = 64
BPS = 16
CAP = 2
NSEC = 16
NBLK = 256


def environment(key):
    first, second = jax.random.split(key)
    diagonal = jnp.exp(jax.random.uniform(first, (NSEC, DW, BS), jnp.float32, 0.0, math.log(3.0)))
    rough = jnp.clip(jax.random.normal(second, (NSEC, DW, BS, BS), jnp.float32), -4.0, 4.0) / math.sqrt(BS)
    marks = (jnp.arange(BS)[:, None] == jnp.arange(BS)[None, :]).astype(jnp.float32)
    return marks * diagonal[..., None] + rough


def draw_left_env(key, part):
    key = jax.random.fold_in(key, 11)
    return environment(key)


def draw_right_env(key, part):
    key = jax.random.fold_in(key, 13)
    return environment(key)


def draw_psi(key, part):
    key = jax.random.fold_in(key, 7)
    first, second = jax.random.split(key)
    places = jnp.arange(NBLK).astype(jnp.float32)
    growth = 3.0 ** (places / max(NBLK - 1, 1))
    scales = jnp.exp(jax.random.uniform(second, (NBLK, BS, 1), jnp.float32, 0.0, math.log(10.0)))
    base = jnp.clip(jax.random.normal(first, (NBLK, BS, BS), jnp.float32), -4.0, 4.0)
    return base * scales * growth[:, None, None]


def draw_right_sector(key, part):
    key = jax.random.fold_in(key, 5)
    first, second, third, fourth = jax.random.split(key, 4)
    sectors = NBLK // BPS
    device = jnp.arange(sectors, dtype=jnp.int32)
    chosen = jax.random.randint(third, (), 1, sectors - 1)
    rising = jnp.where(device == chosen, CAP, jax.random.randint(first, (sectors,), 1, CAP + 1))
    rising = jnp.where(device == sectors - 1, 0, rising)
    falling = jnp.where(device == chosen, CAP, jax.random.randint(second, (sectors,), 1, CAP + 1))
    falling = jnp.where(device == 0, 0, falling)
    slots = jnp.arange(BPS, dtype=jnp.int32)[None, :]
    offsets = jnp.where(slots < rising[:, None], 1, jnp.where(slots < (rising + falling)[:, None], -1, 0))
    scores = jax.random.randint(fourth, (sectors, BPS), 0, 1 << 20) * BPS + slots
    order = jnp.argsort(scores, axis=1, stable=True)
    offsets = jnp.take_along_axis(offsets, order, axis=1)
    return (device[:, None] + offsets).reshape(-1).astype(jnp.int32)


def touch_ends(array, rng, smallest, high):
    shape = array.shape
    place = [jax.random.randint(jax.random.fold_in(rng, axis), (), 0, shape[axis]) for axis in range(len(shape))]
    array = array.at[tuple(place)].set(smallest)
    longest = shape.index(max(shape))
    place[longest] = (place[longest] + 1) % shape[longest]
    return array.at[tuple(place)].set(high)


def setup_inputs(seed: int = 0, part: int = 0) -> dict:
    key_of = jax.random.split(jax.random.key(seed), 7)
    part_keys = jax.random.split(jax.random.fold_in(key_of[6], part), 7)
    psi = draw_psi(jax.random.fold_in(jax.random.fold_in(key_of[6], part), 71), part)
    left_env = draw_left_env(jax.random.fold_in(jax.random.fold_in(key_of[6], part), 71), part)
    right_env = draw_right_env(jax.random.fold_in(jax.random.fold_in(key_of[6], part), 71), part)
    right_sector = draw_right_sector(jax.random.fold_in(jax.random.fold_in(key_of[6], part), 71), part)
    mpo_pairs = touch_ends(jax.random.randint(key_of[4], (NPAIR, 2), 0, DW), jax.random.fold_in(key_of[4], 1), 0, DW - 1).astype(jnp.int32)
    mpo_coef = jnp.clip(jax.random.uniform(key_of[5], (NPAIR,), jnp.float32, 0.0, 0.03125), 0.0, 0.03125)
    return {"psi": psi, "left_env": left_env, "right_env": right_env, "right_sector": right_sector, "mpo_pairs": mpo_pairs, "mpo_coef": mpo_coef}


def reference(psi, left_env, right_env, right_sector, mpo_pairs, mpo_coef):
    highest = lax.Precision.HIGHEST
    coupling = jnp.zeros((DW, DW), jnp.float32).at[mpo_pairs[:, 0], mpo_pairs[:, 1]].add(mpo_coef)

    def one_block(index):
        block = psi[index]
        left = left_env[index // BPS]
        right = right_env[right_sector[index]]
        proj = jnp.einsum("wij,jl->wil", left, block, precision=highest)
        terms = jnp.einsum("wv,wil->vil", coupling, proj, precision=highest)
        return jnp.einsum("vil,vlm->im", terms, right, precision=highest)

    hpsi = lax.map(one_block, jnp.arange(NBLK, dtype=jnp.int32))
    energy = jnp.sum(psi * hpsi) / jnp.sum(psi * psi)
    return hpsi, hpsi - energy * psi
```

```python
import functools
import jax
import jax.numpy as jnp
from jax import lax
from jax.experimental import pallas as pl
from jax.experimental.pallas import tpu as pltpu
from jax.sharding import PartitionSpec as P

CAP = 2
F32 = jnp.float32
BF16 = jnp.bfloat16


def split(x):
    hi = x.astype(BF16)
    return hi, (x - hi.astype(F32)).astype(BF16)


def dot(a, b):
    return jnp.dot(a, b, preferred_element_type=F32)


def kernel(
    n, vc,
    psi_in, left_in, right_in, sector, pairs, coef,
    hpsi_out, res_out,
    psi, left, right, r_hi, r_lo, m_cat, p_cat, r_cat, t_hi, t_lo, off_hi, off_lo,
    acc, hp, res, c_vec, c_sm, part, parts,
    local_sem, up_send, up_recv, dn_send, dn_recv, part_send, part_recv,
):
    nk, bs, _ = psi.shape
    nv = left.shape[0]
    nq = nv // vc
    wide = vc * bs
    me = lax.axis_index("sect")

    loads = [
        pltpu.make_async_copy(left_in.at[0], left, local_sem.at[0]),
        pltpu.make_async_copy(psi_in, psi, local_sem.at[1]),
        pltpu.make_async_copy(right_in.at[0], right, local_sem.at[2]),
    ]
    for c in loads:
        c.start()

    barrier = pltpu.get_barrier_semaphore()

    def greet(d, carry):
        pl.semaphore_signal(
            barrier, inc=1, device_id={"sect": lax.rem(me + d, n)}, device_id_type=pl.DeviceIdType.MESH
        )
        return carry

    lax.fori_loop(1, n, greet, 0)
    pl.semaphore_wait(barrier, n - 1)

    def up_copy(q):
        at = pl.ds(q * vc, vc)
        return pltpu.make_async_remote_copy(
            src_ref=right_in.at[0, at], dst_ref=r_lo.at[at],
            send_sem=up_send.at[q], recv_sem=up_recv.at[q],
            device_id={"sect": me + 1}, device_id_type=pl.DeviceIdType.MESH,
        )

    def dn_copy(q):
        at = pl.ds(q * vc, vc)
        return pltpu.make_async_remote_copy(
            src_ref=right_in.at[0, at], dst_ref=r_hi.at[at],
            send_sem=dn_send.at[q], recv_sem=dn_recv.at[q],
            device_id={"sect": me - 1}, device_id_type=pl.DeviceIdType.MESH,
        )

    has_up = me < n - 1
    has_dn = me > 0
    for q in range(nq):
        @pl.when(has_up)
        def _():
            up_copy(q).start()

        @pl.when(has_dn)
        def _():
            dn_copy(q).start()

    zero = jnp.int32(0)
    picks = [zero] * (2 * CAP)
    n_up = zero
    n_dn = zero
    slots = []
    for k in range(nk):
        offset = sector[k] - me
        up = offset == 1
        dn = offset == -1
        for c in range(CAP):
            picks[c] = jnp.where(up & (n_up == c), k, picks[c])
            picks[CAP + c] = jnp.where(dn & (n_dn == c), k, picks[CAP + c])
        slots.append(jnp.where(up, nk + jnp.minimum(n_up, CAP - 1), jnp.where(dn, nk + CAP + jnp.minimum(n_dn, CAP - 1), k)))
        n_up = n_up + up.astype(jnp.int32)
        n_dn = n_dn + dn.astype(jnp.int32)

    ids = lax.broadcasted_iota(jnp.int32, (pairs.shape[0], 128), 1)
    left_hot = (pairs[:, 0:1] == ids).astype(F32)
    right_hot = jnp.where(pairs[:, 1:2] == ids, coef[...], 0.0)
    coupling = lax.dot_general(
        right_hot, left_hot, (((0,), (0,)), ((), ())),
        precision=lax.Precision.HIGHEST, preferred_element_type=F32,
    )
    c_vec[...] = coupling[:nv]
    c_copy = pltpu.make_async_copy(c_vec, c_sm, local_sem.at[5])
    c_copy.start()
    c_copy.wait()

    acc[...] = jnp.zeros_like(acc)

    loads[0].wait()

    def mix(u, carry):
        total = c_sm[u, 0] * left[0]
        for w in range(1, nv):
            total = total + c_sm[u, w] * left[w]
        hi, lo = split(total)
        m_cat[u, :, 0:bs] = hi
        m_cat[u, :, bs:2 * bs] = lo
        m_cat[u, :, 2 * bs:] = hi
        return carry

    lax.fori_loop(0, nv, mix, 0)

    loads[1].wait()

    def pack_psi(kp, carry):
        for s in range(2):
            hi, lo = split(psi[2 * kp + s])
            lanes = slice(s * bs, (s + 1) * bs)
            p_cat[kp, 0:bs, lanes] = hi
            p_cat[kp, bs:2 * bs, lanes] = hi
            p_cat[kp, 2 * bs:, lanes] = lo
        return carry

    lax.fori_loop(0, nk // 2, pack_psi, 0)
    loads[2].wait()

    def pack_right(u, carry):
        hi, lo = split(right[u])
        r_cat[u, :, 0:bs] = hi
        r_cat[u, :, bs:] = lo
        return carry

    lax.fori_loop(0, nv, pack_right, 0)

    half = nk // 2

    def own(q, carry):
        lhs = m_cat[pl.ds(q * vc, vc)].reshape(wide, 3 * bs)

        def terms(kp, carry):
            hi, lo = split(dot(lhs, p_cat[kp]))
            for v in range(vc):
                rows = slice(v * bs, (v + 1) * bs)
                for s in range(2):
                    lanes = slice(s * bs, (s + 1) * bs)
                    t_hi[2 * kp + s, :, rows] = hi[rows, lanes]
                    t_lo[2 * kp + s, :, rows] = lo[rows, lanes]
            return carry

        lax.fori_loop(0, nk // 2, terms, 0)
        for c in range(2 * CAP):
            off_hi[q, c] = t_hi[picks[c]]
            off_lo[q, c] = t_lo[picks[c]]

        rhs = r_cat[pl.ds(q * vc, vc)].reshape(wide, 2 * bs)

        def close(g, carry):
            at = pl.ds(g * half, half)
            d = dot(t_hi[at].reshape(half * bs, wide), rhs)
            e = dot(t_lo[at].reshape(half * bs, wide), rhs[:, :bs])
            acc[at] += (d[:, :bs] + d[:, bs:] + e).reshape(half, bs, bs)
            return carry

        lax.fori_loop(0, 2, close, 0)
        return carry

    lax.fori_loop(0, nq, own, 0)

    def away(q, carry):
        at = pl.ds(q * vc, vc)

        def add(came, first):
            hi, lo = split(came[at].reshape(wide, bs))
            rows = slice(first, first + CAP)
            a = off_hi[q, rows].reshape(CAP * bs, wide)
            b = off_lo[q, rows].reshape(CAP * bs, wide)
            total = dot(a, hi) + dot(a, lo) + dot(b, hi)
            acc[nk + first:nk + first + CAP] += total.reshape(CAP, bs, bs)

        @pl.when(has_dn)
        def _():
            up_copy(q).wait_recv()
            add(r_lo, CAP)

        @pl.when(has_up)
        def _():
            dn_copy(q).wait_recv()
            add(r_hi, 0)

        return carry

    lax.fori_loop(0, nq, away, 0)

    s1 = jnp.zeros((8, bs), F32)
    s2 = jnp.zeros((8, bs), F32)
    for k in range(nk):
        product = acc[slots[k]]
        block = psi[k]
        hp[k] = product
        s1 = s1 + jnp.sum((block * product).reshape(bs // 8, 8, bs), axis=0)
        s2 = s2 + jnp.sum((block * block).reshape(bs // 8, 8, bs), axis=0)
    part[0:8] = s1
    part[8:16] = s2

    def part_copy(d):
        return pltpu.make_async_remote_copy(
            src_ref=part, dst_ref=parts.at[d],
            send_sem=part_send.at[d], recv_sem=part_recv.at[d],
            device_id={"sect": lax.rem(me + d, n)}, device_id_type=pl.DeviceIdType.MESH,
        )

    def tell(d, carry):
        part_copy(d).start()
        return carry

    lax.fori_loop(1, n, tell, 0)
    hp_copy = pltpu.make_async_copy(hp, hpsi_out, local_sem.at[3])
    hp_copy.start()

    def hear(d, total):
        part_copy(d).wait_recv()
        return total + parts[d]

    total = lax.fori_loop(1, n, hear, part[...])
    energy = jnp.sum(total[0:8], keepdims=True) / jnp.sum(total[8:16], keepdims=True)
    for k in range(nk):
        res[k] = hp[k] - energy * psi[k]
    res_copy = pltpu.make_async_copy(res, res_out, local_sem.at[4])
    res_copy.start()

    def sent(d, carry):
        part_copy(d).wait_send()
        return carry

    lax.fori_loop(1, n, sent, 0)
    for q in range(nq):
        @pl.when(has_up)
        def _():
            up_copy(q).wait_send()

        @pl.when(has_dn)
        def _():
            dn_copy(q).wait_send()

    hp_copy.wait()
    res_copy.wait()


def on_device(n, psi, left_env, right_env, right_sector, mpo_pairs, mpo_coef):
    nk, bs, _ = psi.shape
    nv = left_env.shape[1]
    vc = 8 if nv % 8 == 0 else nv
    nq = nv // vc
    vmem = pltpu.VMEM
    dma = pltpu.SemaphoreType.DMA
    anywhere = pl.BlockSpec(memory_space=pl.ANY)
    return pl.pallas_call(
        functools.partial(kernel, n, vc),
        out_shape=(jax.ShapeDtypeStruct(psi.shape, F32), jax.ShapeDtypeStruct(psi.shape, F32)),
        in_specs=[
            anywhere, anywhere, anywhere,
            pl.BlockSpec(memory_space=pltpu.SMEM),
            pl.BlockSpec(memory_space=vmem),
            pl.BlockSpec(memory_space=vmem),
        ],
        out_specs=(anywhere, anywhere),
        scratch_shapes=[
            vmem((nk, bs, bs), F32),
            vmem((nv, bs, bs), F32),
            vmem((nv, bs, bs), F32),
            vmem((nv, bs, bs), F32),
            vmem((nv, bs, bs), F32),
            vmem((nv, bs, 3 * bs), BF16),
            vmem((nk // 2, 3 * bs, 2 * bs), BF16),
            vmem((nv, bs, 2 * bs), BF16),
            vmem((nk, bs, vc * bs), BF16),
            vmem((nk, bs, vc * bs), BF16),
            vmem((nq, 2 * CAP, bs, vc * bs), BF16),
            vmem((nq, 2 * CAP, bs, vc * bs), BF16),
            vmem((nk + 2 * CAP, bs, bs), F32),
            vmem((nk, bs, bs), F32),
            vmem((nk, bs, bs), F32),
            vmem((nv, 128), F32),
            pltpu.SMEM((nv, 128), F32),
            vmem((16, bs), F32),
            vmem((n, 16, bs), F32),
            dma((6,)),
            dma((nq,)), dma((nq,)), dma((nq,)), dma((nq,)),
            dma((n,)), dma((n,)),
        ],
        compiler_params=pltpu.CompilerParams(
            collective_id=0, has_side_effects=True, vmem_limit_bytes=56 * 1024 * 1024
        ),
    )(psi, left_env, right_env, right_sector, mpo_pairs, mpo_coef[:, None])


def solution(mesh):
    in_specs = (
        P(("groups", "sect"), None, None),
        P(("groups", "sect"), None, None, None),
        P(("groups", "sect"), None, None, None),
        P(("groups", "sect")),
        P(),
        P(),
    )
    out_specs = (P(("groups", "sect"), None, None), P(("groups", "sect"), None, None))
    return jax.shard_map(
        functools.partial(on_device, mesh.shape["sect"]),
        mesh=mesh, in_specs=in_specs, out_specs=out_specs, check_vma=False,
    )
```

```python
import functools
import jax
import jax.numpy as jnp
from jax import lax
from jax.experimental import pallas as pl
from jax.experimental.pallas import tpu as pltpu
from jax.sharding import PartitionSpec as P

CAP = 2
F32 = jnp.float32
BF16 = jnp.bfloat16


def split(x):
    hi = x.astype(BF16)
    return hi, (x - hi.astype(F32)).astype(BF16)


def dot(a, b):
    return jnp.dot(a, b, preferred_element_type=F32)


def kernel(
    n, vc, xc,
    psi_in, left_in, right_in, sector, pairs, coef,
    hpsi_out, energy_out,
    psi, left, right, r_hi, r_lo, m_cat, p_cat, r_cat, t_hi, t_lo, off_hi, off_lo,
    acc, hp, c_vec, c_sm, part, parts,
    local_sem, up_send, up_recv, dn_send, dn_recv, part_send, part_recv,
):
    nk, bs, _ = psi.shape
    nv = left.shape[0]
    nq = nv // vc
    nx = nv // xc
    per = vc // xc
    wide = vc * bs
    narrow = xc * bs
    me = lax.axis_index("sect")

    loads = [
        pltpu.make_async_copy(left_in.at[0], left, local_sem.at[0]),
        pltpu.make_async_copy(psi_in, psi, local_sem.at[1]),
        pltpu.make_async_copy(right_in.at[0], right, local_sem.at[2]),
    ]
    for c in loads:
        c.start()

    barrier = pltpu.get_barrier_semaphore()

    def greet(d, carry):
        pl.semaphore_signal(
            barrier, inc=1, device_id={"sect": lax.rem(me + d, n)}, device_id_type=pl.DeviceIdType.MESH
        )
        return carry

    lax.fori_loop(1, n, greet, 0)
    pl.semaphore_wait(barrier, n - 1)

    def up_copy(q):
        at = pl.ds(q * xc, xc)
        return pltpu.make_async_remote_copy(
            src_ref=right_in.at[0, at], dst_ref=r_lo.at[at],
            send_sem=up_send.at[q], recv_sem=up_recv.at[q],
            device_id={"sect": me + 1}, device_id_type=pl.DeviceIdType.MESH,
        )

    def dn_copy(q):
        at = pl.ds(q * xc, xc)
        return pltpu.make_async_remote_copy(
            src_ref=right_in.at[0, at], dst_ref=r_hi.at[at],
            send_sem=dn_send.at[q], recv_sem=dn_recv.at[q],
            device_id={"sect": me - 1}, device_id_type=pl.DeviceIdType.MESH,
        )

    has_up = me < n - 1
    has_dn = me > 0
    from_up, from_dn = has_up, has_dn
    for q in range(nx):
        @pl.when(has_up)
        def _():
            up_copy(q).start()

        @pl.when(has_dn)
        def _():
            dn_copy(q).start()

    zero = jnp.int32(0)
    picks = [zero] * (2 * CAP)
    n_up = zero
    n_dn = zero
    slots = []
    for k in range(nk):
        offset = sector[k] - me
        up = offset == 1
        dn = offset == -1
        for c in range(CAP):
            picks[c] = jnp.where(up & (n_up == c), k, picks[c])
            picks[CAP + c] = jnp.where(dn & (n_dn == c), k, picks[CAP + c])
        slots.append(jnp.where(up, nk + jnp.minimum(n_up, CAP - 1), jnp.where(dn, nk + CAP + jnp.minimum(n_dn, CAP - 1), k)))
        n_up = n_up + up.astype(jnp.int32)
        n_dn = n_dn + dn.astype(jnp.int32)

    ids = lax.broadcasted_iota(jnp.int32, (128, pairs.shape[1]), 0)
    left_hot = (pairs[0:1, :] == ids).astype(F32)
    right_hot = jnp.where(pairs[1:2, :] == ids, coef[...], 0.0)
    coupling = lax.dot_general(
        right_hot, left_hot, (((1,), (1,)), ((), ())),
        precision=lax.Precision.HIGHEST, preferred_element_type=F32,
    )
    c_vec[...] = coupling[:nv]
    c_copy = pltpu.make_async_copy(c_vec, c_sm, local_sem.at[5])
    c_copy.start()
    c_copy.wait()

    acc[...] = jnp.zeros_like(acc)

    loads[0].wait()

    def mix(u, carry):
        total = c_sm[u, 0] * left[0]
        for w in range(1, nv):
            total = total + c_sm[u, w] * left[w]
        hi, lo = split(total)
        m_cat[u, :, 0:bs] = hi
        m_cat[u, :, bs:2 * bs] = lo
        m_cat[u, :, 2 * bs:] = hi
        return carry

    lax.fori_loop(0, nv, mix, 0)

    loads[1].wait()

    def pack_psi(kp, carry):
        for s in range(2):
            hi, lo = split(psi[2 * kp + s])
            lanes = slice(s * bs, (s + 1) * bs)
            p_cat[kp, 0:bs, lanes] = hi
            p_cat[kp, bs:2 * bs, lanes] = hi
            p_cat[kp, 2 * bs:, lanes] = lo
        return carry

    lax.fori_loop(0, nk // 2, pack_psi, 0)
    loads[2].wait()

    def pack_right(u, carry):
        hi, lo = split(right[u])
        r_cat[u, :, 0:bs] = hi
        r_cat[u, :, bs:] = lo
        return carry

    lax.fori_loop(0, nv, pack_right, 0)

    half = nk // 2

    def own(q, carry):
        lhs = m_cat[pl.ds(q * vc, vc)].reshape(wide, 3 * bs)

        def terms(kp, carry):
            hi, lo = split(dot(lhs, p_cat[kp]))
            for v in range(vc):
                rows = slice(v * bs, (v + 1) * bs)
                for s in range(2):
                    lanes = slice(s * bs, (s + 1) * bs)
                    t_hi[2 * kp + s, :, rows] = hi[rows, lanes]
                    t_lo[2 * kp + s, :, rows] = lo[rows, lanes]
            return carry

        lax.fori_loop(0, nk // 2, terms, 0)
        for c in range(2 * CAP):
            hi, lo = t_hi[picks[c]], t_lo[picks[c]]
            for h in range(per):
                off_hi[q * per + h, c] = hi[:, h * narrow:(h + 1) * narrow]
                off_lo[q * per + h, c] = lo[:, h * narrow:(h + 1) * narrow]

        rhs = r_cat[pl.ds(q * vc, vc)].reshape(wide, 2 * bs)

        def close(g, carry):
            at = pl.ds(g * half, half)
            d = dot(t_hi[at].reshape(half * bs, wide), rhs)
            e = dot(t_lo[at].reshape(half * bs, wide), rhs[:, :bs])
            acc[at] += (d[:, :bs] + d[:, bs:] + e).reshape(half, bs, bs)
            return carry

        lax.fori_loop(0, 2, close, 0)
        return carry

    lax.fori_loop(0, nq, own, 0)

    def lines(x):
        return jnp.sum(x.reshape(bs // 8, 8, bs), axis=0)

    s1 = jnp.zeros((8, bs), F32)
    s2 = jnp.zeros((8, bs), F32)
    for k in range(nk):
        block = psi[k]
        s1 = s1 + jnp.where(slots[k] == k, lines(block * acc[k]), 0.0)
        s2 = s2 + lines(block * block)

    def away(q, carry):
        at = pl.ds(q * xc, xc)

        def add(came, first):
            hi, lo = split(came[at].reshape(narrow, bs))
            rows = slice(first, first + CAP)
            a = off_hi[q, rows].reshape(CAP * bs, narrow)
            b = off_lo[q, rows].reshape(CAP * bs, narrow)
            total = dot(a, hi) + dot(a, lo) + dot(b, hi)
            acc[nk + first:nk + first + CAP] += total.reshape(CAP, bs, bs)

        @pl.when(from_dn)
        def _():
            up_copy(q).wait_recv()
            add(r_lo, CAP)

        @pl.when(from_up)
        def _():
            dn_copy(q).wait_recv()
            add(r_hi, 0)

        return carry

    lax.fori_loop(0, nx, away, 0)

    for c in range(CAP):
        s1 = s1 + jnp.where(n_up > c, lines(psi[picks[c]] * acc[nk + c]), 0.0)
        s1 = s1 + jnp.where(n_dn > c, lines(psi[picks[CAP + c]] * acc[nk + CAP + c]), 0.0)
    part[0:4] = s1[0:4] + s1[4:8]
    part[4:8] = s2[0:4] + s2[4:8]

    def part_copy(d):
        return pltpu.make_async_remote_copy(
            src_ref=part, dst_ref=parts.at[d],
            send_sem=part_send.at[d], recv_sem=part_recv.at[d],
            device_id={"sect": lax.rem(me + d, n)}, device_id_type=pl.DeviceIdType.MESH,
        )

    def tell(d, carry):
        part_copy(d).start()
        return carry

    lax.fori_loop(1, n, tell, 0)
    for k in range(nk):
        hp[k] = acc[slots[k]]
    hp_copy = pltpu.make_async_copy(hp, hpsi_out, local_sem.at[3])
    hp_copy.start()

    def hear(d, total):
        part_copy(d).wait_recv()
        return total + parts[d]

    total = lax.fori_loop(1, n, hear, part[...])
    energy = jnp.sum(total[0:4], keepdims=True) / jnp.sum(total[4:8], keepdims=True)
    energy_out[...] = jnp.broadcast_to(energy, (8, bs))

    def sent(d, carry):
        part_copy(d).wait_send()
        return carry

    lax.fori_loop(1, n, sent, 0)
    for q in range(nx):
        @pl.when(has_up)
        def _():
            up_copy(q).wait_send()

        @pl.when(has_dn)
        def _():
            dn_copy(q).wait_send()

    hp_copy.wait()


def finish(hp, psi, energy, hpsi_out, res_out):
    x = hp[...]
    hpsi_out[...] = x
    res_out[...] = x - energy[0:1, :][None] * psi[...]


def on_device(n, psi, left_env, right_env, right_sector, mpo_pairs, mpo_coef):
    nk, bs, _ = psi.shape
    nv = left_env.shape[1]
    vc = 8 if nv % 8 == 0 else nv
    xc = 4 if nv % 8 == 0 else nv
    nx = nv // xc
    vmem = pltpu.VMEM
    dma = pltpu.SemaphoreType.DMA
    anywhere = pl.BlockSpec(memory_space=pl.ANY)
    product, energy = pl.pallas_call(
        functools.partial(kernel, n, vc, xc),
        out_shape=(jax.ShapeDtypeStruct(psi.shape, F32), jax.ShapeDtypeStruct((8, bs), F32)),
        in_specs=[
            anywhere, anywhere, anywhere,
            pl.BlockSpec(memory_space=pltpu.SMEM),
            pl.BlockSpec(memory_space=vmem),
            pl.BlockSpec(memory_space=vmem),
        ],
        out_specs=(anywhere, pl.BlockSpec(memory_space=vmem)),
        scratch_shapes=[
            vmem((nk, bs, bs), F32),
            vmem((nv, bs, bs), F32),
            vmem((nv, bs, bs), F32),
            vmem((nv, bs, bs), F32),
            vmem((nv, bs, bs), F32),
            vmem((nv, bs, 3 * bs), BF16),
            vmem((nk // 2, 3 * bs, 2 * bs), BF16),
            vmem((nv, bs, 2 * bs), BF16),
            vmem((nk, bs, vc * bs), BF16),
            vmem((nk, bs, vc * bs), BF16),
            vmem((nx, 2 * CAP, bs, xc * bs), BF16),
            vmem((nx, 2 * CAP, bs, xc * bs), BF16),
            vmem((nk + 2 * CAP, bs, bs), F32),
            vmem((nk, bs, bs), F32),
            vmem((nv, 128), F32),
            pltpu.SMEM((nv, 128), F32),
            vmem((8, bs), F32),
            vmem((n, 8, bs), F32),
            dma((6,)),
            dma((nx,)), dma((nx,)), dma((nx,)), dma((nx,)),
            dma((n,)), dma((n,)),
        ],
        compiler_params=pltpu.CompilerParams(
            collective_id=0, has_side_effects=True, vmem_limit_bytes=56 * 1024 * 1024
        ),
    )(psi, left_env, right_env, right_sector, mpo_pairs.T, mpo_coef[None, :])
    step = nk // 4
    blocks = pl.BlockSpec((step, bs, bs), lambda i: (i, 0, 0))
    return pl.pallas_call(
        finish,
        grid=(nk // step,),
        out_shape=(jax.ShapeDtypeStruct(psi.shape, F32), jax.ShapeDtypeStruct(psi.shape, F32)),
        in_specs=[blocks, blocks, pl.BlockSpec((8, bs), lambda i: (0, 0))],
        out_specs=(blocks, blocks),
    )(product, psi, energy)


def solution(mesh):
    in_specs = (
        P(("groups", "sect"), None, None),
        P(("groups", "sect"), None, None, None),
        P(("groups", "sect"), None, None, None),
        P(("groups", "sect")),
        P(),
        P(),
    )
    out_specs = (P(("groups", "sect"), None, None), P(("groups", "sect"), None, None))
    return jax.shard_map(
        functools.partial(on_device, mesh.shape["sect"]),
        mesh=mesh, in_specs=in_specs, out_specs=out_specs, check_vma=False,
    )
```

```python
import functools
import jax
import jax.numpy as jnp
from jax import lax
from jax.experimental import pallas as pl
from jax.experimental.pallas import tpu as pltpu
from jax.sharding import PartitionSpec as P

CAP = 2
F32 = jnp.float32
BF16 = jnp.bfloat16


def split(x):
    hi = x.astype(BF16)
    return hi, (x - hi.astype(F32)).astype(BF16)


def dot(a, b):
    return jnp.dot(a, b, preferred_element_type=F32)


def kernel(
    n, vc, xc,
    psi_in, left_in, right_in, sector, pairs, coef,
    hpsi_out, energy_out,
    psi, left, right, r_hi, r_lo, m_cat, p_cat, r_cat, t_hi, t_lo, off_hi, off_lo,
    acc, hp, hold, c_cat, part, parts,
    local_sem, hold_send, hold_recv, up_send, up_recv, dn_send, dn_recv, part_send, part_recv,
):
    nk, bs, _ = psi.shape
    nv = left.shape[0]
    nq = nv // vc
    nx = nv // xc
    per = vc // xc
    wide = vc * bs
    narrow = xc * bs
    me = lax.axis_index("sect")

    loads = [
        pltpu.make_async_copy(left_in.at[0], left, local_sem.at[0]),
        pltpu.make_async_copy(psi_in, psi, local_sem.at[1]),
        pltpu.make_async_copy(right_in.at[0], right, local_sem.at[2]),
    ]
    for c in loads:
        c.start()

    barrier = pltpu.get_barrier_semaphore()

    def greet(d, carry):
        pl.semaphore_signal(
            barrier, inc=1, device_id={"sect": lax.rem(me + d, n)}, device_id_type=pl.DeviceIdType.MESH
        )
        return carry

    lax.fori_loop(1, n, greet, 0)
    pl.semaphore_wait(barrier, n - 1)

    def send(src, dst, q, send_sem, recv_sem, to):
        at = pl.ds(q * xc, xc)
        return pltpu.make_async_remote_copy(
            src_ref=src.at[at], dst_ref=dst.at[at],
            send_sem=send_sem.at[q], recv_sem=recv_sem.at[q],
            device_id={"sect": to}, device_id_type=pl.DeviceIdType.MESH,
        )

    mine = right_in.at[0]

    def up_copy(q):
        return send(mine, r_lo, q, up_send, up_recv, me + 1)

    def dn_copy(q):
        return send(mine, r_hi, q, dn_send, dn_recv, me - 1)

    rows = n // 4 if n % 4 == 0 else 1
    row, place = lax.div(me, 4), lax.rem(me, 4)
    zero = jnp.int32(0)
    by_up = lax.div(nx * (rows - 1 - row), rows) if rows > 1 else zero
    by_dn = lax.div(nx * row, rows) if rows > 1 else zero
    up_count = jnp.where(place == 3, by_up, 0)
    dn_count = jnp.where(place == 0, by_dn, 0)
    hand_up = jnp.where(place == 1, by_up, 0)
    hand_dn = jnp.where(place == 2, by_dn, 0)

    def forward(i):
        @pl.when(i < hand_up)
        def _():
            q = nx - hand_up + i
            send(mine, hold, q, up_send, hold_recv, lax.rem(me + 1, n)).wait_recv()
            send(hold, r_lo, q, hold_send, up_recv, me + 3).start()

        @pl.when(i < hand_dn)
        def _():
            q = nx - hand_dn + i
            send(mine, hold, q, dn_send, hold_recv, lax.rem(me + 1, n)).wait_recv()
            send(hold, r_hi, q, hold_send, dn_recv, me - 3).start()

    has_up = me < n - 1
    has_dn = me > 0
    from_up, from_dn = has_up, has_dn
    for i in range(nx):
        @pl.when(i < up_count)
        def _():
            send(mine, hold, nx - up_count + i, up_send, hold_recv, me - 2).start()

        @pl.when(i < dn_count)
        def _():
            send(mine, hold, nx - dn_count + i, dn_send, hold_recv, me + 2).start()

    for q in range(nx):
        @pl.when(has_up & (q < nx - up_count))
        def _():
            up_copy(q).start()

        @pl.when(has_dn & (q < nx - dn_count))
        def _():
            dn_copy(q).start()

    picks = [zero] * (2 * CAP)
    n_up = zero
    n_dn = zero
    slots = []
    for k in range(nk):
        offset = sector[k] - me
        up = offset == 1
        dn = offset == -1
        for c in range(CAP):
            picks[c] = jnp.where(up & (n_up == c), k, picks[c])
            picks[CAP + c] = jnp.where(dn & (n_dn == c), k, picks[CAP + c])
        slots.append(jnp.where(up, nk + jnp.minimum(n_up, CAP - 1), jnp.where(dn, nk + CAP + jnp.minimum(n_dn, CAP - 1), k)))
        n_up = n_up + up.astype(jnp.int32)
        n_dn = n_dn + dn.astype(jnp.int32)

    size = 8 * nv
    ids = lax.div(lax.broadcasted_iota(jnp.int32, (size, pairs.shape[1]), 0), 8)
    left_hot = (pairs[0:1, :] == ids).astype(F32)
    right_hot = jnp.where(pairs[1:2, :] == ids, coef[...], 0.0)
    coupling = lax.dot_general(
        right_hot, left_hot, (((1,), (1,)), ((), ())),
        precision=lax.Precision.HIGHEST, preferred_element_type=F32,
    )
    here = lax.rem(lax.broadcasted_iota(jnp.int32, (size, size), 0), 8)
    there = lax.rem(lax.broadcasted_iota(jnp.int32, (size, size), 1), 8)
    c_hi, c_lo = split(jnp.where(here == there, coupling, 0.0))
    c_cat[0] = c_hi
    c_cat[1] = c_lo

    acc[...] = jnp.zeros_like(acc)

    loads[0].wait()

    def mix(g, carry):
        at = pl.multiple_of(g * 16, 16)
        strip = jnp.concatenate(
            [left[:, pl.ds(at, 8), :].reshape(size, bs), left[:, pl.ds(at + 8, 8), :].reshape(size, bs)], axis=1
        )
        l_hi, l_lo = split(strip)
        total = dot(c_cat[0], l_hi) + dot(c_cat[0], l_lo) + dot(c_cat[1], l_hi)
        both = jnp.concatenate([total[:, :bs].reshape(nv, 8, bs), total[:, bs:].reshape(nv, 8, bs)], axis=1)
        hi, lo = split(both)
        m_cat[:, pl.ds(at, 16), 0:bs] = hi
        m_cat[:, pl.ds(at, 16), bs:2 * bs] = lo
        m_cat[:, pl.ds(at, 16), 2 * bs:] = hi
        return carry

    lax.fori_loop(0, bs // 16, mix, 0)

    loads[1].wait()

    def pack_psi(kp, carry):
        for s in range(2):
            hi, lo = split(psi[2 * kp + s])
            lanes = slice(s * bs, (s + 1) * bs)
            p_cat[kp, 0:bs, lanes] = hi
            p_cat[kp, bs:2 * bs, lanes] = hi
            p_cat[kp, 2 * bs:, lanes] = lo
        return carry

    lax.fori_loop(0, nk // 2, pack_psi, 0)
    loads[2].wait()

    def pack_right(u, carry):
        hi, lo = split(right[u])
        r_cat[u, :, 0:bs] = hi
        r_cat[u, :, bs:] = lo
        return carry

    lax.fori_loop(0, nv, pack_right, 0)

    half = nk // 2

    def own(q, carry):
        lhs = m_cat[pl.ds(q * vc, vc)].reshape(wide, 3 * bs)

        def terms(kp, carry):
            hi, lo = split(dot(lhs, p_cat[kp]))
            for v in range(vc):
                rows = slice(v * bs, (v + 1) * bs)
                for s in range(2):
                    lanes = slice(s * bs, (s + 1) * bs)
                    t_hi[2 * kp + s, :, rows] = hi[rows, lanes]
                    t_lo[2 * kp + s, :, rows] = lo[rows, lanes]
            return carry

        lax.fori_loop(0, nk // 2, terms, 0)
        forward(q)
        for c in range(2 * CAP):
            hi, lo = t_hi[picks[c]], t_lo[picks[c]]
            for h in range(per):
                off_hi[q * per + h, c] = hi[:, h * narrow:(h + 1) * narrow]
                off_lo[q * per + h, c] = lo[:, h * narrow:(h + 1) * narrow]

        rhs = r_cat[pl.ds(q * vc, vc)].reshape(wide, 2 * bs)

        def close(g, carry):
            at = pl.ds(g * half, half)
            d = dot(t_hi[at].reshape(half * bs, wide), rhs)
            e = dot(t_lo[at].reshape(half * bs, wide), rhs[:, :bs])
            acc[at] += (d[:, :bs] + d[:, bs:] + e).reshape(half, bs, bs)
            return carry

        lax.fori_loop(0, 2, close, 0)
        return carry

    lax.fori_loop(0, nq, own, 0)
    for i in range(nq, nx):
        forward(i)

    def lines(x):
        return jnp.sum(x.reshape(bs // 8, 8, bs), axis=0)

    s1 = jnp.zeros((8, bs), F32)
    s2 = jnp.zeros((8, bs), F32)
    for k in range(nk):
        block = psi[k]
        s1 = s1 + jnp.where(slots[k] == k, lines(block * acc[k]), 0.0)
        s2 = s2 + lines(block * block)

    def away(q, carry):
        at = pl.ds(q * xc, xc)

        def add(came, first):
            hi, lo = split(came[at].reshape(narrow, bs))
            rows = slice(first, first + CAP)
            a = off_hi[q, rows].reshape(CAP * bs, narrow)
            b = off_lo[q, rows].reshape(CAP * bs, narrow)
            total = dot(a, hi) + dot(a, lo) + dot(b, hi)
            acc[nk + first:nk + first + CAP] += total.reshape(CAP, bs, bs)

        @pl.when(from_dn)
        def _():
            up_copy(q).wait_recv()
            add(r_lo, CAP)

        @pl.when(from_up)
        def _():
            dn_copy(q).wait_recv()
            add(r_hi, 0)

        return carry

    lax.fori_loop(0, nx, away, 0)

    for c in range(CAP):
        s1 = s1 + jnp.where(n_up > c, lines(psi[picks[c]] * acc[nk + c]), 0.0)
        s1 = s1 + jnp.where(n_dn > c, lines(psi[picks[CAP + c]] * acc[nk + CAP + c]), 0.0)
    part[0:4] = s1[0:4] + s1[4:8]
    part[4:8] = s2[0:4] + s2[4:8]

    def part_copy(d):
        return pltpu.make_async_remote_copy(
            src_ref=part, dst_ref=parts.at[d],
            send_sem=part_send.at[d], recv_sem=part_recv.at[d],
            device_id={"sect": lax.rem(me + d, n)}, device_id_type=pl.DeviceIdType.MESH,
        )

    def tell(d, carry):
        part_copy(d).start()
        return carry

    lax.fori_loop(1, n, tell, 0)
    for k in range(nk):
        hp[k] = acc[slots[k]]
    hp_copy = pltpu.make_async_copy(hp, hpsi_out, local_sem.at[3])
    hp_copy.start()

    def hear(d, total):
        part_copy(d).wait_recv()
        return total + parts[d]

    total = lax.fori_loop(1, n, hear, part[...])
    energy = jnp.sum(total[0:4], keepdims=True) / jnp.sum(total[4:8], keepdims=True)
    energy_out[...] = jnp.broadcast_to(energy, (8, bs))

    def sent(d, carry):
        part_copy(d).wait_send()
        return carry

    lax.fori_loop(1, n, sent, 0)
    for q in range(nx):
        @pl.when(has_up)
        def _():
            up_copy(q).wait_send()

        @pl.when(has_dn)
        def _():
            dn_copy(q).wait_send()

    for q in range(nx):
        @pl.when(q >= nx - hand_up - hand_dn)
        def _():
            send(hold, r_lo, q, hold_send, up_recv, lax.rem(me + 1, n)).wait_send()

    hp_copy.wait()


def finish(parts, hp_in, psi_in, energy, hpsi_out, res_out, hp, psi, res, in_sem, out_sem):
    step = hp.shape[0] // parts
    at = [pl.ds(i * step, step) for i in range(parts)]
    loads = [
        (pltpu.make_async_copy(hp_in.at[a], hp.at[a], in_sem.at[0, i]), pltpu.make_async_copy(psi_in.at[a], psi.at[a], in_sem.at[1, i]))
        for i, a in enumerate(at)
    ]
    stores = [
        (pltpu.make_async_copy(hp.at[a], hpsi_out.at[a], out_sem.at[0, i]), pltpu.make_async_copy(res.at[a], res_out.at[a], out_sem.at[1, i]))
        for i, a in enumerate(at)
    ]
    for first, second in loads:
        first.start()
        second.start()
    quotient = energy[0:1, :][None]
    for i, a in enumerate(at):
        loads[i][0].wait()
        stores[i][0].start()
        loads[i][1].wait()
        res[a] = hp[a] - quotient * psi[a]
        stores[i][1].start()
    for first, second in stores:
        first.wait()
        second.wait()


def on_device(n, psi, left_env, right_env, right_sector, mpo_pairs, mpo_coef):
    nk, bs, _ = psi.shape
    nv = left_env.shape[1]
    vc = 8 if nv % 8 == 0 else nv
    xc = 4 if nv % 8 == 0 else nv
    nx = nv // xc
    vmem = pltpu.VMEM
    dma = pltpu.SemaphoreType.DMA
    anywhere = pl.BlockSpec(memory_space=pl.ANY)
    product, energy = pl.pallas_call(
        functools.partial(kernel, n, vc, xc),
        out_shape=(jax.ShapeDtypeStruct(psi.shape, F32), jax.ShapeDtypeStruct((8, bs), F32)),
        in_specs=[
            anywhere, anywhere, anywhere,
            pl.BlockSpec(memory_space=pltpu.SMEM),
            pl.BlockSpec(memory_space=vmem),
            pl.BlockSpec(memory_space=vmem),
        ],
        out_specs=(anywhere, pl.BlockSpec(memory_space=vmem)),
        scratch_shapes=[
            vmem((nk, bs, bs), F32),
            vmem((nv, bs, bs), F32),
            vmem((nv, bs, bs), F32),
            vmem((nv, bs, bs), F32),
            vmem((nv, bs, bs), F32),
            vmem((nv, bs, 3 * bs), BF16),
            vmem((nk // 2, 3 * bs, 2 * bs), BF16),
            vmem((nv, bs, 2 * bs), BF16),
            vmem((nk, bs, vc * bs), BF16),
            vmem((nk, bs, vc * bs), BF16),
            vmem((nx, 2 * CAP, bs, xc * bs), BF16),
            vmem((nx, 2 * CAP, bs, xc * bs), BF16),
            vmem((nk + 2 * CAP, bs, bs), F32),
            vmem((nk, bs, bs), F32),
            vmem((nv, bs, bs), F32),
            vmem((2, 8 * nv, 8 * nv), BF16),
            vmem((8, bs), F32),
            vmem((n, 8, bs), F32),
            dma((4,)),
            dma((nx,)), dma((nx,)), dma((nx,)), dma((nx,)), dma((nx,)), dma((nx,)),
            dma((n,)), dma((n,)),
        ],
        compiler_params=pltpu.CompilerParams(
            collective_id=0, has_side_effects=True, vmem_limit_bytes=56 * 1024 * 1024
        ),
    )(psi, left_env, right_env, right_sector, mpo_pairs.T, mpo_coef[None, :])
    return pl.pallas_call(
        functools.partial(finish, 4),
        out_shape=(jax.ShapeDtypeStruct(psi.shape, F32), jax.ShapeDtypeStruct(psi.shape, F32)),
        in_specs=[anywhere, anywhere, pl.BlockSpec(memory_space=vmem)],
        out_specs=(anywhere, anywhere),
        scratch_shapes=[vmem(psi.shape, F32), vmem(psi.shape, F32), vmem(psi.shape, F32), dma((2, 4)), dma((2, 4))],
    )(product, psi, energy)


def solution(mesh):
    in_specs = (
        P(("groups", "sect"), None, None),
        P(("groups", "sect"), None, None, None),
        P(("groups", "sect"), None, None, None),
        P(("groups", "sect")),
        P(),
        P(),
    )
    out_specs = (P(("groups", "sect"), None, None), P(("groups", "sect"), None, None))
    return jax.shard_map(
        functools.partial(on_device, mesh.shape["sect"]),
        mesh=mesh, in_specs=in_specs, out_specs=out_specs, check_vma=False,
    )
```
